512 devices in a mesh: queue: 32 (over y_lo, x, core), space: 16 (over y_hi, z).
Axes of the slice: x: 4, y: 8 (y_hi: 2, y_lo: 4; y = y_hi * 4 + y_lo), z: 8, core: 2. Of those that a mesh axis runs over, the one named last changes fastest.
Arguments:
- residual: bfloat16 [32, 3600, 2048], P('queue', 'space'), may hold values from -6 to 6
- head_queries: bfloat16 [32, 3600, 2048], P('queue', 'space'), may hold values from -11 to 11
- head_keys: bfloat16 [32, 3600, 2048], P('queue', 'space'), may hold values from -11 to 11
- head_values: bfloat16 [32, 3600, 2048], P('queue', 'space'), may hold values from -6 to 6
- levels: int32 [32], P('queue'), may hold values from 0 to 63, as said below
- window: int32 [32, 2], P('queue'), may hold values from 0 to 1
- level_gate: float32 [64, 2048], replicated, may hold values from 0.25 to 2
- fresh_frame: bfloat16 [3600, 2048], P('space'), may hold values from -6 to 6
Outputs:
- advanced: bfloat16 [32, 3600, 2048], P('queue', 'space')
The draws below stay inside these ranges and needn't reach their ends.
Inputs may be any that keep to these rules, and one draw needn't show every extreme that they name: `levels`: frame f has level 2 f or 2 f + 1; the first frame has level 0 and the last 63.
All inputs are finite; a program needn't handle non-finite values.
Results may differ from the reference program's by a relative error of at most 0.004.
Values may be sent and summed in bfloat16 or wider, within the bound.
No kernel may reach another device: no remote copies, remote signals or barrier semaphores. Data moves between devices by JAX's collectives and lax.ppermute only.
A program may use at most 64 MiB of HBM per device.

```python
import math
import jax
import jax.numpy as jnp
from jax import lax

HEADS = 16
HEAD_DIM = 128
REACH = 1
CHANNELS = 2048
TOKF = 3600
FRAMES = 32
LEVELS = 64


def draw_head_queries(key, part):
    key = jax.random.fold_in(key, 11)
    return jax.random.truncated_normal(key, -4.0, 4.0, (FRAMES, TOKF, CHANNELS), jnp.float32).astype(jnp.bfloat16)


def draw_head_keys(key, part):
    key = jax.random.fold_in(key, 13)
    background = 1.5 * jax.random.truncated_normal(key, -4.0, 4.0, (FRAMES, TOKF, CHANNELS), jnp.float32)
    return background.astype(jnp.bfloat16)


def draw_levels(key, part):
    key = jax.random.fold_in(key, 37)
    frames = jnp.arange(FRAMES, dtype=jnp.int32)
    levels = 2 * frames + jax.random.randint(key, (FRAMES,), 0, 2, jnp.int32)
    return levels.at[0].set(0).at[FRAMES - 1].set(LEVELS - 1)


def draw_window(key, part):
    key = jax.random.fold_in(key, 23)
    offsets_drawn = jax.random.randint(key, (FRAMES, 2), 0, REACH + 1, jnp.int32)
    middle = FRAMES // 2
    offsets_drawn = offsets_drawn.at[middle - 1].set(REACH).at[middle].set(REACH).at[middle + 1].set(REACH)
    return offsets_drawn.at[FRAMES - 1].set(0)


def steps_of(key, dims, pieces, least, high):
    def one(axis_at, shards_of):
        heights = jax.random.uniform(jax.random.fold_in(jax.random.fold_in(key, 6), axis_at), (shards_of,), jnp.float32, least / len(pieces), high / len(pieces))
        return jnp.repeat(jnp.exp(heights), dims[axis_at] // shards_of).reshape((-1,) + (1,) * (len(dims) - axis_at - 1))

    level = one(*pieces[0])
    for cut in pieces[1:]:
        level = level * one(*cut)
    return level


def bell_draw(stream_key, shape, spread, reach, pieces=(), kind=jnp.bfloat16):
    drawn = spread * jax.random.normal(stream_key, shape, jnp.float32)
    if pieces:
        drawn = drawn * steps_of(stream_key, shape, pieces, -0.22, 0.18)
    return jnp.clip(drawn, -reach, reach).astype(kind)


def setup_inputs(seed: int = 0) -> dict:
    streams_of = jax.random.split(jax.random.key(seed), 9)
    return {
        "residual": bell_draw(streams_of[0], (FRAMES, TOKF, CHANNELS), 1.0, 6.0, ((0, 32), (1, 16))),
        "head_queries": draw_head_queries(jax.random.fold_in(streams_of[8], 71), 0),
        "head_keys": draw_head_keys(jax.random.fold_in(streams_of[8], 71), 0),
        "head_values": bell_draw(streams_of[3], (FRAMES, TOKF, CHANNELS), 1.0, 6.0, ((0, 32), (1, 16))),
        "levels": draw_levels(jax.random.fold_in(streams_of[8], 71), 0),
        "window": draw_window(jax.random.fold_in(streams_of[8], 71), 0),
        "level_gate": jnp.clip(jnp.exp(jax.random.uniform(streams_of[6], (LEVELS, CHANNELS), jnp.float32, math.log(0.25), math.log(2.0))), 0.25, 2.0),
        "fresh_frame": bell_draw(streams_of[7], (TOKF, CHANNELS), 1.0, 6.0, ((0, 16),)),
    }


masked_score = -1e+30

def spatial_frame(query_frame, key_frame, value_frame):
    scaling = 1.0 / math.sqrt(HEAD_DIM)
    query_heads = query_frame.reshape(TOKF, HEADS, HEAD_DIM).transpose(1, 0, 2)
    key_heads = key_frame.reshape(TOKF, HEADS, HEAD_DIM).transpose(1, 0, 2)
    value_heads = value_frame.reshape(TOKF, HEADS, HEAD_DIM).transpose(1, 0, 2)

    def one_head(operands):
        query_one, key_one, value_one = operands
        scores = jnp.dot(query_one, key_one.T, preferred_element_type=jnp.float32) * scaling
        row_top = lax.optimization_barrier(jnp.max(scores, axis=1, keepdims=True))
        expo_terms = jnp.exp(scores - row_top)
        row_total = lax.optimization_barrier(jnp.sum(expo_terms, axis=1, keepdims=True))
        summed = jnp.dot(expo_terms.astype(jnp.bfloat16), value_one, preferred_element_type=jnp.float32)
        return (summed / row_total).astype(jnp.bfloat16)
    out_heads = lax.map(one_head, (query_heads, key_heads, value_heads))
    return out_heads.transpose(1, 0, 2).reshape(TOKF, CHANNELS)

def temporal_frame(frame_index, query_frame, padded_keys, padded_values, reach_back, reach_ahead):
    scaling = 1.0 / math.sqrt(HEAD_DIM)
    window_span = 2 * REACH + 1
    near_keys = lax.dynamic_slice_in_dim(padded_keys, frame_index, window_span, 0)
    near_values = lax.dynamic_slice_in_dim(padded_values, frame_index, window_span, 0)
    query_heads = query_frame.astype(jnp.float32).reshape(TOKF, HEADS, HEAD_DIM)
    key_heads = near_keys.astype(jnp.float32).reshape(window_span, TOKF, HEADS, HEAD_DIM)
    value_heads = near_values.astype(jnp.float32).reshape(window_span, TOKF, HEADS, HEAD_DIM)
    scores = jnp.einsum('thd,jthd->jth', query_heads, key_heads) * scaling
    offsets = jnp.arange(window_span, dtype=jnp.int32) - REACH
    target = frame_index + offsets
    usable = (offsets >= -reach_back) & (offsets <= reach_ahead) & (target >= 0) & (target < FRAMES)
    scores = jnp.where(usable[:, None, None], scores, masked_score)
    row_top = lax.optimization_barrier(jnp.max(scores, axis=0))
    expo_terms = jnp.exp(scores - row_top[None])
    row_total = lax.optimization_barrier(jnp.sum(expo_terms, axis=0))
    weights = lax.optimization_barrier(expo_terms.astype(jnp.bfloat16)).astype(jnp.float32)
    summed = jnp.einsum('jth,jthd->thd', weights, value_heads)
    return (summed / row_total[..., None]).reshape(TOKF, CHANNELS)

def reference(residual, head_queries, head_keys, head_values, levels, window, level_gate, fresh_frame):
    padding = jnp.zeros((REACH, TOKF, CHANNELS), jnp.bfloat16)
    padded_keys = jnp.concatenate([padding, head_keys, padding], axis=0)
    padded_values = jnp.concatenate([padding, head_values, padding], axis=0)

    def one_frame(frame_index):
        spatial = spatial_frame(head_queries[frame_index], head_keys[frame_index], head_values[frame_index])
        temporal = temporal_frame(frame_index, head_queries[frame_index], padded_keys, padded_values, window[frame_index, 0], window[frame_index, 1])
        spatial_wide = lax.optimization_barrier(spatial).astype(jnp.float32)
        mixed_out = (spatial_wide + temporal).astype(jnp.bfloat16)
        mixed_wide = lax.optimization_barrier(mixed_out).astype(jnp.float32)
        chooser = (jnp.arange(LEVELS, dtype=jnp.int32) == levels[frame_index]).astype(jnp.float32)
        gate_row = jnp.dot(chooser[None], level_gate, precision=lax.Precision.HIGHEST)[0]
        return (residual[frame_index].astype(jnp.float32) + gate_row[None] * mixed_wide).astype(jnp.bfloat16)
    updated = lax.map(one_frame, jnp.arange(1, FRAMES, dtype=jnp.int32))
    return jnp.concatenate([updated, fresh_frame[None]], axis=0)
```

```python
import functools
import math

import jax
import jax.numpy as jnp
from jax import lax
from jax.experimental import pallas as pl
from jax.experimental.pallas import tpu as pltpu
from jax.sharding import PartitionSpec as P

HEAD_DIM = 128
SCALE = 1.0 / math.sqrt(HEAD_DIM)
LOG2E = 1.4426950408889634
MASKED = -1e30
MIB = 1024 * 1024


def pack_kernel(q_ref, k_ref, v_ref, out_ref, *, main):
    for part, ref in enumerate((q_ref, k_ref, v_ref)):
        out_ref[0, part * main : (part + 1) * main, :] = ref[0, :main, :]
    row = lax.broadcasted_iota(jnp.int32, (16, HEAD_DIM), 0)
    tail = jnp.zeros((16, HEAD_DIM), jnp.float32)
    for part, ref in enumerate((q_ref, k_ref, v_ref)):
        last = ref[0, main : main + 1, :].astype(jnp.float32)
        tail = jnp.where(row == part, last, tail)
    out_ref[0, 3 * main :, :] = tail.astype(jnp.bfloat16)


def pack(queries, keys, values):
    _, rows, channels = queries.shape
    heads = channels // HEAD_DIM
    main = rows - 1
    total = 3 * main + 16
    spec = pl.BlockSpec((1, rows, HEAD_DIM), lambda h: (0, 0, h))
    return pl.pallas_call(
        functools.partial(pack_kernel, main=main),
        grid=(heads,),
        in_specs=[spec] * 3,
        out_specs=pl.BlockSpec((1, total, HEAD_DIM), lambda h: (h, 0, 0)),
        out_shape=jax.ShapeDtypeStruct((heads, total, HEAD_DIM), jnp.bfloat16),
        cost_estimate=pl.CostEstimate(flops=0, bytes_accessed=6 * queries.size * 2, transcendentals=0),
        name="pack",
    )(queries, keys, values)


def attend_kernel(got_ref, out_ref, q_all, k_all, v_all, o_all, *, sources, main, block):
    row = lax.broadcasted_iota(jnp.int32, (16, HEAD_DIM), 0)
    tails = [jnp.zeros((16, HEAD_DIM), jnp.float32) for _ in range(3)]
    for s in range(sources):
        at = slice(s * main, (s + 1) * main)
        q_all[at, :] = got_ref[s, :main, :]
        k_all[at, :] = got_ref[s, main : 2 * main, :]
        v_all[at, :HEAD_DIM] = got_ref[s, 2 * main : 3 * main, :]
        tail = got_ref[s, 3 * main :, :].astype(jnp.float32)
        for part in range(3):
            tails[part] = jnp.where(row == s, tail[part : part + 1, :], tails[part])
    end = sources * main
    q_all[end:, :] = tails[0].astype(jnp.bfloat16)
    k_all[end:, :] = tails[1].astype(jnp.bfloat16)
    v_all[end:, :HEAD_DIM] = tails[2].astype(jnp.bfloat16)
    v_all[:, HEAD_DIM:] = jnp.ones((end + 16, HEAD_DIM), jnp.bfloat16)

    def one_block(i, carry):
        rows = pl.ds(pl.multiple_of(i * block, 16), block)
        scores = lax.dot_general(
            q_all[rows, :], k_all[...], (((1,), (1,)), ((), ())), preferred_element_type=jnp.float32
        )
        top = jnp.max(scores, axis=1, keepdims=True)
        weights = jnp.exp2((scores - top) * (SCALE * LOG2E)).astype(jnp.bfloat16)
        summed = jnp.dot(weights, v_all[...], preferred_element_type=jnp.float32)
        o_all[rows, :] = (summed[:, :HEAD_DIM] / summed[:, HEAD_DIM:]).astype(jnp.bfloat16)
        return carry

    lax.fori_loop(0, (end + 16) // block, one_block, 0)
    last = o_all[end:, :].astype(jnp.float32)
    for s in range(sources):
        out_ref[s, :main, :] = o_all[s * main : (s + 1) * main, :]
        out_ref[s, main : main + 1, :] = last[s : s + 1, :].astype(jnp.bfloat16)


def attend(got, rows):
    sources, total, _ = got.shape
    main = rows - 1
    tokens = sources * rows
    block = 400
    return pl.pallas_call(
        functools.partial(attend_kernel, sources=sources, main=main, block=block),
        in_specs=[pl.BlockSpec(memory_space=pltpu.VMEM)],
        out_specs=pl.BlockSpec(memory_space=pltpu.VMEM),
        out_shape=jax.ShapeDtypeStruct((sources, rows, HEAD_DIM), jnp.bfloat16),
        scratch_shapes=[
            pltpu.VMEM((tokens, HEAD_DIM), jnp.bfloat16),
            pltpu.VMEM((tokens, HEAD_DIM), jnp.bfloat16),
            pltpu.VMEM((tokens, 2 * HEAD_DIM), jnp.bfloat16),
            pltpu.VMEM((tokens, HEAD_DIM), jnp.bfloat16),
        ],
        compiler_params=pltpu.CompilerParams(vmem_limit_bytes=48 * MIB),
        cost_estimate=pl.CostEstimate(
            flops=4 * tokens * tokens * HEAD_DIM, bytes_accessed=8 * tokens * HEAD_DIM, transcendentals=tokens * tokens
        ),
        name="attend",
    )(got)


def temporal_kernel(usable_ref, q_ref, k0, k1, k2, v0, v1, v2, out_ref):
    q = q_ref[0].astype(jnp.float32)
    scores = []
    for j, ref in enumerate((k0, k1, k2)):
        score = jnp.sum(q * ref[0].astype(jnp.float32), axis=1, keepdims=True) * SCALE
        scores.append(jnp.where(usable_ref[j] > 0, score, MASKED))
    top = jnp.maximum(jnp.maximum(scores[0], scores[1]), scores[2])
    terms = [jnp.exp(score - top) for score in scores]
    total = terms[0] + terms[1] + terms[2]
    summed = jnp.zeros_like(q)
    for term, ref in zip(terms, (v0, v1, v2)):
        summed += term.astype(jnp.bfloat16).astype(jnp.float32) * ref[0].astype(jnp.float32)
    out_ref[0] = summed / total


def temporal_attend(usable, queries, near_keys, near_values):
    _, rows, channels = queries.shape
    spec = pl.BlockSpec((1, rows, HEAD_DIM), lambda h: (0, 0, h))
    return pl.pallas_call(
        temporal_kernel,
        grid=(channels // HEAD_DIM,),
        in_specs=[pl.BlockSpec(memory_space=pltpu.SMEM)] + [spec] * 7,
        out_specs=spec,
        out_shape=jax.ShapeDtypeStruct(queries.shape, jnp.float32),
        cost_estimate=pl.CostEstimate(flops=12 * queries.size, bytes_accessed=18 * queries.size, transcendentals=0),
        name="temporal",
    )(usable, queries, *near_keys, *near_values)


def finish_kernel(first_ref, spatial_ref, temporal_ref, residual_ref, gate_ref, fresh_ref, out_ref):
    mixed = (spatial_ref[0].astype(jnp.float32) + temporal_ref[0]).astype(jnp.bfloat16)
    updated = residual_ref[0].astype(jnp.float32) + gate_ref[...] * mixed.astype(jnp.float32)
    is_first = first_ref[0] > 0
    out_ref[0] = jnp.where(is_first, fresh_ref[...].astype(jnp.float32), updated).astype(jnp.bfloat16)


def finish(is_first, spatial, temporal, residual, gate_row, fresh):
    heads, rows, _ = spatial.shape
    by_head = pl.BlockSpec((1, rows, HEAD_DIM), lambda h: (0, 0, h))
    return pl.pallas_call(
        finish_kernel,
        grid=(heads,),
        in_specs=[
            pl.BlockSpec(memory_space=pltpu.SMEM),
            pl.BlockSpec((1, rows, HEAD_DIM), lambda h: (h, 0, 0)),
            by_head,
            by_head,
            pl.BlockSpec((1, HEAD_DIM), lambda h: (0, h)),
            pl.BlockSpec((rows, HEAD_DIM), lambda h: (0, h)),
        ],
        out_specs=by_head,
        out_shape=jax.ShapeDtypeStruct(residual.shape, jnp.bfloat16),
        cost_estimate=pl.CostEstimate(flops=4 * residual.size, bytes_accessed=12 * residual.size, transcendentals=0),
        name="finish",
    )(is_first, spatial, temporal, residual, gate_row, fresh)


def on_device(residual, head_queries, head_keys, head_values, levels, window, level_gate, fresh_frame):
    rows = head_queries.shape[1]
    frame = lax.axis_index("queue")
    frames = lax.axis_size("queue")
    up = [(i, i + 1) for i in range(frames - 1)]
    down = [(j, i) for i, j in up]

    sent = pack(head_queries, head_keys, head_values)
    got = lax.all_to_all(sent, "space", split_axis=0, concat_axis=0, tiled=True)

    near_keys = (lax.ppermute(head_keys, "queue", up), head_keys, lax.ppermute(head_keys, "queue", down))
    near_values = (lax.ppermute(head_values, "queue", up), head_values, lax.ppermute(head_values, "queue", down))
    before = (window[0, 0] >= 1) & (frame >= 1)
    after = (window[0, 1] >= 1) & (frame <= frames - 2)
    usable = jnp.stack([before, jnp.bool_(True), after]).astype(jnp.int32)
    temporal = temporal_attend(usable, head_queries, near_keys, near_values)

    back = attend(got, rows)
    spatial = lax.all_to_all(back, "space", split_axis=0, concat_axis=0, tiled=True)
    gate_row = lax.dynamic_slice_in_dim(level_gate, levels[0], 1, axis=0)
    is_first = (frame == 0).astype(jnp.int32)[None]
    updated = finish(is_first, spatial, temporal, residual, gate_row, fresh_frame)
    return lax.ppermute(updated, "queue", [(i, (i - 1) % frames) for i in range(frames)])


def solution(mesh):
    placed = (
        P("queue", "space", None),
        P("queue", "space", None),
        P("queue", "space", None),
        P("queue", "space", None),
        P("queue"),
        P("queue", None),
        P(),
        P("space", None),
    )
    return jax.shard_map(
        on_device, mesh=mesh, in_specs=placed, out_specs=P("queue", "space", None), check_vma=False
    )
```

```python
import functools
import math

import jax
import jax.numpy as jnp
from jax import lax
from jax.experimental import pallas as pl
from jax.experimental.pallas import tpu as pltpu
from jax.sharding import PartitionSpec as P

HEAD_DIM = 128
SCALE = 1.0 / math.sqrt(HEAD_DIM)
LOG2E = 1.4426950408889634
MASKED = -1e30
MIB = 1024 * 1024
STEP_HEADS = 4
QUERY_BLOCK = 720
KEY_BLOCK = 720


def columns(head):
    return slice(head * HEAD_DIM, (head + 1) * HEAD_DIM)


def pack_kernel(q_ref, k_ref, v_ref, out_ref, own_ref, *, main):
    for part, ref in enumerate((k_ref, v_ref)):
        own_ref[part, main:, :] = jnp.zeros_like(own_ref[part, main:, :])
        own_ref[part, : main + 1, :] = ref[0]
    row = lax.broadcasted_iota(jnp.int32, (16, HEAD_DIM), 0)
    for head in range(STEP_HEADS):
        tail = jnp.zeros((16, HEAD_DIM), jnp.float32)
        for part, ref in enumerate((q_ref, k_ref, v_ref)):
            out_ref[head, part * main : (part + 1) * main, :] = ref[0, :main, columns(head)]
            last = ref[0, main : main + 1, columns(head)].astype(jnp.float32)
            tail = jnp.where(row == part, last, tail)
        out_ref[head, 3 * main :, :] = tail.astype(jnp.bfloat16)


def pack(queries, keys, values):
    _, rows, channels = queries.shape
    heads = channels // HEAD_DIM
    main = rows - 1
    total = 3 * main + 16
    spec = pl.BlockSpec((1, rows, STEP_HEADS * HEAD_DIM), lambda h: (0, 0, h))
    return pl.pallas_call(
        functools.partial(pack_kernel, main=main),
        grid=(heads // STEP_HEADS,),
        in_specs=[spec] * 3,
        out_specs=[
            pl.BlockSpec((STEP_HEADS, total, HEAD_DIM), lambda h: (h, 0, 0)),
            pl.BlockSpec((2, main + 16, STEP_HEADS * HEAD_DIM), lambda h: (0, 0, h)),
        ],
        out_shape=[
            jax.ShapeDtypeStruct((heads, total, HEAD_DIM), jnp.bfloat16),
            jax.ShapeDtypeStruct((2, main + 16, channels), jnp.bfloat16),
        ],
        cost_estimate=pl.CostEstimate(flops=0, bytes_accessed=8 * queries.size * 2, transcendentals=0),
        name="pack",
    )(queries, keys, values)


def attend_kernel(got_ref, out_ref, q_all, k_all, v_all, o_all, *, sources, main):
    row = lax.broadcasted_iota(jnp.int32, (16, HEAD_DIM), 0)
    tails = [jnp.zeros((16, HEAD_DIM), jnp.float32) for _ in range(3)]
    for s in range(sources):
        at = slice(s * main, (s + 1) * main)
        q_all[at, :] = got_ref[s, :main, :]
        k_all[at, :] = got_ref[s, main : 2 * main, :]
        v_all[at, :HEAD_DIM] = got_ref[s, 2 * main : 3 * main, :]
        tail = got_ref[s, 3 * main :, :].astype(jnp.float32)
        for part in range(3):
            tails[part] = jnp.where(row == s, tail[part : part + 1, :], tails[part])
    end = sources * main
    q_all[end:, :] = tails[0].astype(jnp.bfloat16)
    k_all[end:, :] = tails[1].astype(jnp.bfloat16)
    v_all[end:, :HEAD_DIM] = tails[2].astype(jnp.bfloat16)
    v_all[:, HEAD_DIM:] = jnp.ones((end + 16, HEAD_DIM), jnp.bfloat16)

    def one_block(i, carry):
        rows = pl.ds(pl.multiple_of(i * QUERY_BLOCK, 16), QUERY_BLOCK)
        queries = q_all[rows, :]
        top = summed = None
        for start in range(0, end + 16, KEY_BLOCK):
            keys = slice(start, start + KEY_BLOCK)
            scores = lax.dot_general(
                queries, k_all[keys, :], (((1,), (1,)), ((), ())), preferred_element_type=jnp.float32
            )
            here = jnp.max(scores, axis=1, keepdims=True)
            new_top = here if top is None else jnp.maximum(top, here)
            weights = jnp.exp2((scores - new_top) * (SCALE * LOG2E)).astype(jnp.bfloat16)
            part = jnp.dot(weights, v_all[keys, :], preferred_element_type=jnp.float32)
            summed = part if top is None else summed * jnp.exp2((top - new_top) * (SCALE * LOG2E)) + part
            top = new_top
        o_all[rows, :] = (summed[:, :HEAD_DIM] / summed[:, HEAD_DIM:]).astype(jnp.bfloat16)
        return carry

    lax.fori_loop(0, (end + 16) // QUERY_BLOCK, one_block, 0, unroll=True)
    last = o_all[end:, :].astype(jnp.float32)
    for s in range(sources):
        out_ref[s, :main, :] = o_all[s * main : (s + 1) * main, :]
        out_ref[s, main : main + 1, :] = last[s : s + 1, :].astype(jnp.bfloat16)


def attend(got, rows):
    sources, total, _ = got.shape
    main = rows - 1
    tokens = sources * rows
    return pl.pallas_call(
        functools.partial(attend_kernel, sources=sources, main=main),
        in_specs=[pl.BlockSpec(memory_space=pltpu.VMEM)],
        out_specs=pl.BlockSpec(memory_space=pltpu.VMEM),
        out_shape=jax.ShapeDtypeStruct((sources, rows, HEAD_DIM), jnp.bfloat16),
        scratch_shapes=[
            pltpu.VMEM((tokens, HEAD_DIM), jnp.bfloat16),
            pltpu.VMEM((tokens, HEAD_DIM), jnp.bfloat16),
            pltpu.VMEM((tokens, 2 * HEAD_DIM), jnp.bfloat16),
            pltpu.VMEM((tokens, HEAD_DIM), jnp.bfloat16),
        ],
        compiler_params=pltpu.CompilerParams(vmem_limit_bytes=48 * MIB),
        cost_estimate=pl.CostEstimate(
            flops=4 * tokens * tokens * HEAD_DIM, bytes_accessed=8 * tokens * HEAD_DIM, transcendentals=tokens * tokens
        ),
        name="attend",
    )(got)


def temporal_kernel(usable_ref, q_ref, k_ref, v_ref, before_ref, after_ref, out_ref):
    rows = q_ref.shape[1]
    for head in range(STEP_HEADS):
        at = columns(head)
        q = q_ref[0, :, at].astype(jnp.float32)
        keys = (before_ref[0, :rows, at], k_ref[0, :, at], after_ref[0, :rows, at])
        values = (before_ref[1, :rows, at], v_ref[0, :, at], after_ref[1, :rows, at])
        scores = []
        for j in range(3):
            score = jnp.sum(q * keys[j].astype(jnp.float32), axis=1, keepdims=True) * SCALE
            scores.append(jnp.where(usable_ref[j] > 0, score, MASKED))
        top = jnp.maximum(jnp.maximum(scores[0], scores[1]), scores[2])
        terms = [jnp.exp(score - top) for score in scores]
        total = terms[0] + terms[1] + terms[2]
        summed = jnp.zeros_like(q)
        for j in range(3):
            summed += terms[j].astype(jnp.bfloat16).astype(jnp.float32) * values[j].astype(jnp.float32)
        out_ref[0, :, at] = summed / total


def temporal_attend(usable, queries, keys, values, before, after):
    _, rows, channels = queries.shape
    width = STEP_HEADS * HEAD_DIM
    spec = pl.BlockSpec((1, rows, width), lambda h: (0, 0, h))
    pair = pl.BlockSpec((2, before.shape[1], width), lambda h: (0, 0, h))
    return pl.pallas_call(
        temporal_kernel,
        grid=(channels // width,),
        in_specs=[pl.BlockSpec(memory_space=pltpu.SMEM), spec, spec, spec, pair, pair],
        out_specs=spec,
        out_shape=jax.ShapeDtypeStruct(queries.shape, jnp.float32),
        cost_estimate=pl.CostEstimate(flops=12 * queries.size, bytes_accessed=18 * queries.size, transcendentals=0),
        name="temporal",
    )(usable, queries, keys, values, before, after)


def finish_kernel(first_ref, spatial_ref, temporal_ref, residual_ref, gate_ref, fresh_ref, out_ref):
    is_first = first_ref[0] > 0
    for head in range(STEP_HEADS):
        at = columns(head)
        mixed = (spatial_ref[head].astype(jnp.float32) + temporal_ref[0, :, at]).astype(jnp.bfloat16)
        updated = residual_ref[0, :, at].astype(jnp.float32) + gate_ref[:, at] * mixed.astype(jnp.float32)
        fresh = fresh_ref[:, at].astype(jnp.float32)
        out_ref[0, :, at] = jnp.where(is_first, fresh, updated).astype(jnp.bfloat16)


def finish(is_first, spatial, temporal, residual, gate_row, fresh):
    heads, rows, _ = spatial.shape
    width = STEP_HEADS * HEAD_DIM
    by_head = pl.BlockSpec((1, rows, width), lambda h: (0, 0, h))
    return pl.pallas_call(
        finish_kernel,
        grid=(heads // STEP_HEADS,),
        in_specs=[
            pl.BlockSpec(memory_space=pltpu.SMEM),
            pl.BlockSpec((STEP_HEADS, rows, HEAD_DIM), lambda h: (h, 0, 0)),
            by_head,
            by_head,
            pl.BlockSpec((1, width), lambda h: (0, h)),
            pl.BlockSpec((rows, width), lambda h: (0, h)),
        ],
        out_specs=by_head,
        out_shape=jax.ShapeDtypeStruct(residual.shape, jnp.bfloat16),
        cost_estimate=pl.CostEstimate(flops=4 * residual.size, bytes_accessed=12 * residual.size, transcendentals=0),
        name="finish",
    )(is_first, spatial, temporal, residual, gate_row, fresh)


def on_device(residual, head_queries, head_keys, head_values, levels, window, level_gate, fresh_frame):
    rows = head_queries.shape[1]
    frame = lax.axis_index("queue")
    frames = lax.axis_size("queue")
    up = [(i, i + 1) for i in range(frames - 1)]
    down = [(j, i) for i, j in up]

    sent, own = pack(head_queries, head_keys, head_values)
    got = lax.all_to_all(sent, "space", split_axis=0, concat_axis=0, tiled=True)

    before = (window[0, 0] >= 1) & (frame >= 1)
    after = (window[0, 1] >= 1) & (frame <= frames - 2)
    usable = jnp.stack([before, jnp.bool_(True), after]).astype(jnp.int32)
    gate_row = lax.dynamic_slice_in_dim(level_gate, levels[0], 1, axis=0)
    is_first = (frame == 0).astype(jnp.int32)[None]

    got, own = lax.optimization_barrier((got, own))
    from_before = lax.ppermute(own, "queue", up)
    from_after = lax.ppermute(own, "queue", down)
    back = attend(got, rows)
    back, from_before, from_after = lax.optimization_barrier((back, from_before, from_after))
    temporal = temporal_attend(usable, head_queries, head_keys, head_values, from_before, from_after)
    spatial = lax.all_to_all(back, "space", split_axis=0, concat_axis=0, tiled=True)
    updated = finish(is_first, spatial, temporal, residual, gate_row, fresh_frame)
    return lax.ppermute(updated, "queue", [(i, (i - 1) % frames) for i in range(frames)])


def solution(mesh):
    placed = (
        P("queue", "space", None),
        P("queue", "space", None),
        P("queue", "space", None),
        P("queue", "space", None),
        P("queue"),
        P("queue", None),
        P(),
        P("space", None),
    )
    return jax.shard_map(
        on_device, mesh=mesh, in_specs=placed, out_specs=P("queue", "space", None), check_vma=False
    )
```

```python
import functools
import math

import jax
import jax.numpy as jnp
from jax import lax
from jax.experimental import pallas as pl
from jax.experimental.pallas import tpu as pltpu
from jax.sharding import PartitionSpec as P

HEAD_DIM = 128
SCALE = 1.0 / math.sqrt(HEAD_DIM)
LOG2E = 1.4426950408889634
MASKED = -1e30
MIB = 1024 * 1024
STEP_HEADS = 4
TAIL = 8
QUERY_BLOCK = 720
KEY_BLOCK = 720


def columns(head):
    return slice(head * HEAD_DIM, (head + 1) * HEAD_DIM)


def pack_kernel(q_ref, k_ref, v_ref, out_ref, own_ref, *, main):
    for part, ref in enumerate((k_ref, v_ref)):
        own_ref[part, main:, :] = jnp.zeros_like(own_ref[part, main:, :])
        own_ref[part, : main + 1, :] = ref[0]
    row = lax.broadcasted_iota(jnp.int32, (TAIL, HEAD_DIM), 0)
    for head in range(STEP_HEADS):
        tail = jnp.zeros((TAIL, HEAD_DIM), jnp.float32)
        for part, ref in enumerate((q_ref, k_ref, v_ref)):
            out_ref[head, part * main : (part + 1) * main, :] = ref[0, :main, columns(head)]
            last = ref[0, main : main + 1, columns(head)].astype(jnp.float32)
            tail = jnp.where(row == part, last, tail)
        out_ref[head, 3 * main :, :] = tail.astype(jnp.bfloat16)


def pack(queries, keys, values):
    _, rows, channels = queries.shape
    heads = channels // HEAD_DIM
    main = rows - 1
    total = 3 * main + TAIL
    spec = pl.BlockSpec((1, rows, STEP_HEADS * HEAD_DIM), lambda h: (0, 0, h))
    return pl.pallas_call(
        functools.partial(pack_kernel, main=main),
        grid=(heads // STEP_HEADS,),
        in_specs=[spec] * 3,
        out_specs=[
            pl.BlockSpec((STEP_HEADS, total, HEAD_DIM), lambda h: (h, 0, 0)),
            pl.BlockSpec((2, main + 8, STEP_HEADS * HEAD_DIM), lambda h: (0, 0, h)),
        ],
        out_shape=[
            jax.ShapeDtypeStruct((heads, total, HEAD_DIM), jnp.bfloat16),
            jax.ShapeDtypeStruct((2, main + 8, channels), jnp.bfloat16),
        ],
        cost_estimate=pl.CostEstimate(flops=0, bytes_accessed=8 * queries.size * 2, transcendentals=0),
        name="pack",
    )(queries, keys, values)


def attend_kernel(got_ref, out_ref, q_all, k_all, v_all, o_all, *, sources, main):
    row = lax.broadcasted_iota(jnp.int32, (16, HEAD_DIM), 0)
    tails = [jnp.zeros((16, HEAD_DIM), jnp.float32) for _ in range(3)]
    for s in range(sources):
        at = slice(s * main, (s + 1) * main)
        q_all[at, :] = got_ref[s, :main, :]
        k_all[at, :] = got_ref[s, main : 2 * main, :]
        v_all[at, :HEAD_DIM] = got_ref[s, 2 * main : 3 * main, :]
        tail = got_ref[s, 3 * main :, :].astype(jnp.float32)
        for part in range(3):
            tails[part] = jnp.where(row == s, tail[part : part + 1, :], tails[part])
    end = sources * main
    q_all[end:, :] = tails[0].astype(jnp.bfloat16)
    k_all[end:, :] = tails[1].astype(jnp.bfloat16)
    v_all[end:, :HEAD_DIM] = tails[2].astype(jnp.bfloat16)
    v_all[:, HEAD_DIM:] = jnp.ones((end + 16, HEAD_DIM), jnp.bfloat16)

    def one_block(i, carry):
        rows = pl.ds(pl.multiple_of(i * QUERY_BLOCK, 16), QUERY_BLOCK)
        queries = q_all[rows, :]
        top = summed = None
        for start in range(0, end + 16, KEY_BLOCK):
            keys = slice(start, start + KEY_BLOCK)
            scores = lax.dot_general(
                queries, k_all[keys, :], (((1,), (1,)), ((), ())), preferred_element_type=jnp.float32
            )
            here = jnp.max(scores, axis=1, keepdims=True)
            new_top = here if top is None else jnp.maximum(top, here)
            weights = jnp.exp2((scores - new_top) * (SCALE * LOG2E)).astype(jnp.bfloat16)
            part = jnp.dot(weights, v_all[keys, :], preferred_element_type=jnp.float32)
            summed = part if top is None else summed * jnp.exp2((top - new_top) * (SCALE * LOG2E)) + part
            top = new_top
        o_all[rows, :] = (summed[:, :HEAD_DIM] / summed[:, HEAD_DIM:]).astype(jnp.bfloat16)
        return carry

    lax.fori_loop(0, (end + 16) // QUERY_BLOCK, one_block, 0, unroll=True)
    last = o_all[end:, :].astype(jnp.float32)
    for s in range(sources):
        out_ref[s, :main, :] = o_all[s * main : (s + 1) * main, :]
        out_ref[s, main : main + 1, :] = last[s : s + 1, :].astype(jnp.bfloat16)


def attend(got, rows):
    sources, total, _ = got.shape
    main = rows - 1
    tokens = sources * rows
    return pl.pallas_call(
        functools.partial(attend_kernel, sources=sources, main=main),
        in_specs=[pl.BlockSpec(memory_space=pltpu.VMEM)],
        out_specs=pl.BlockSpec(memory_space=pltpu.VMEM),
        out_shape=jax.ShapeDtypeStruct((sources, rows, HEAD_DIM), jnp.bfloat16),
        scratch_shapes=[
            pltpu.VMEM((tokens, HEAD_DIM), jnp.bfloat16),
            pltpu.VMEM((tokens, HEAD_DIM), jnp.bfloat16),
            pltpu.VMEM((tokens, 2 * HEAD_DIM), jnp.bfloat16),
            pltpu.VMEM((tokens, HEAD_DIM), jnp.bfloat16),
        ],
        compiler_params=pltpu.CompilerParams(vmem_limit_bytes=48 * MIB),
        cost_estimate=pl.CostEstimate(
            flops=4 * tokens * tokens * HEAD_DIM, bytes_accessed=8 * tokens * HEAD_DIM, transcendentals=tokens * tokens
        ),
        name="attend",
    )(got)


def temporal_kernel(usable_ref, q_ref, k_ref, v_ref, near_k_ref, near_v_ref, far_ref, out_ref):
    rows = q_ref.shape[1]
    for head in range(STEP_HEADS):
        at = columns(head)
        q = q_ref[0, :, at].astype(jnp.float32)
        keys = (k_ref[0, :, at], near_k_ref[0, :, at], far_ref[0, :rows, at])
        values = (v_ref[0, :, at], near_v_ref[0, :, at], far_ref[1, :rows, at])
        scores = []
        for j in range(3):
            score = jnp.sum(q * keys[j].astype(jnp.float32), axis=1, keepdims=True) * SCALE
            scores.append(jnp.where(usable_ref[j] > 0, score, MASKED))
        top = jnp.maximum(jnp.maximum(scores[0], scores[1]), scores[2])
        terms = [jnp.exp(score - top) for score in scores]
        total = terms[0] + terms[1] + terms[2]
        summed = jnp.zeros_like(q)
        for j in range(3):
            summed += terms[j].astype(jnp.bfloat16).astype(jnp.float32) * values[j].astype(jnp.float32)
        out_ref[0, :, at] = summed / total


def temporal_attend(usable, queries, keys, values, near_keys, near_values, far):
    _, rows, channels = queries.shape
    width = STEP_HEADS * HEAD_DIM
    spec = pl.BlockSpec((1, rows, width), lambda h: (0, 0, h))
    pair = pl.BlockSpec((2, far.shape[1], width), lambda h: (0, 0, h))
    return pl.pallas_call(
        temporal_kernel,
        grid=(channels // width,),
        in_specs=[pl.BlockSpec(memory_space=pltpu.SMEM)] + [spec] * 5 + [pair],
        out_specs=spec,
        out_shape=jax.ShapeDtypeStruct(queries.shape, jnp.float32),
        cost_estimate=pl.CostEstimate(flops=12 * queries.size, bytes_accessed=18 * queries.size, transcendentals=0),
        name="temporal",
    )(usable, queries, keys, values, near_keys, near_values, far)


def finish_kernel(first_ref, spatial_ref, temporal_ref, residual_ref, gate_ref, fresh_ref, out_ref):
    is_first = first_ref[0] > 0
    for head in range(spatial_ref.shape[0]):
        at = columns(head)
        mixed = (spatial_ref[head].astype(jnp.float32) + temporal_ref[0, :, at]).astype(jnp.bfloat16)
        updated = residual_ref[0, :, at].astype(jnp.float32) + gate_ref[:, at] * mixed.astype(jnp.float32)
        out_ref[0, :, at] = jnp.where(is_first, fresh_ref[:, at].astype(jnp.float32), updated).astype(jnp.bfloat16)


def finish(is_first, spatial, temporal, residual, gate_row, fresh):
    return pl.pallas_call(
        finish_kernel,
        in_specs=[pl.BlockSpec(memory_space=pltpu.SMEM)] + [pl.BlockSpec(memory_space=pltpu.VMEM)] * 5,
        out_specs=pl.BlockSpec(memory_space=pltpu.VMEM),
        out_shape=jax.ShapeDtypeStruct(residual.shape, jnp.bfloat16),
        compiler_params=pltpu.CompilerParams(vmem_limit_bytes=16 * MIB),
        cost_estimate=pl.CostEstimate(flops=4 * residual.size, bytes_accessed=12 * residual.size, transcendentals=0),
        name="finish",
    )(is_first, spatial, temporal, residual, gate_row, fresh)


def on_device(residual, head_queries, head_keys, head_values, levels, window, level_gate, fresh_frame):
    rows = head_queries.shape[1]
    frame = lax.axis_index("queue")
    frames = lax.axis_size("queue")
    near_pairs = [(i, i ^ 1) for i in range(frames)]
    far_pairs = [(i, j) for i, j in ((i, ((i + 1) ^ 1) - 1) for i in range(frames)) if 0 <= j < frames]

    sent, own = pack(head_queries, head_keys, head_values)
    got = lax.all_to_all(sent, "space", split_axis=0, concat_axis=0, tiled=True)
    got, own, window, levels = lax.optimization_barrier((got, own, window, levels))

    far = lax.ppermute(own, "queue", far_pairs)
    before = (window[0, 0] >= 1) & (frame >= 1)
    after = (window[0, 1] >= 1) & (frame <= frames - 2)
    odd = frame % 2 == 1
    near_usable, far_usable = jnp.where(odd, before, after), jnp.where(odd, after, before)
    usable = jnp.stack([jnp.bool_(True), near_usable, far_usable]).astype(jnp.int32)
    is_first = (frame == 0).astype(jnp.int32)[None]
    gate_row = lax.dynamic_slice_in_dim(level_gate, levels[0], 1, axis=0)
    back = attend(got, rows)
    back, far, head_keys, head_values = lax.optimization_barrier((back, far, head_keys, head_values))

    near_keys = lax.ppermute(head_keys, "queue", near_pairs)
    near_values = lax.ppermute(head_values, "queue", near_pairs)
    temporal = temporal_attend(usable, head_queries, head_keys, head_values, near_keys, near_values, far)
    spatial = lax.all_to_all(back, "space", split_axis=0, concat_axis=0, tiled=True)
    updated = finish(is_first, spatial, temporal, residual, gate_row, fresh_frame)
    return lax.ppermute(updated, "queue", [(i, (i - 1) % frames) for i in range(frames)])


def solution(mesh):
    placed = (
        P("queue", "space", None),
        P("queue", "space", None),
        P("queue", "space", None),
        P("queue", "space", None),
        P("queue"),
        P("queue", None),
        P(),
        P("space", None),
    )
    return jax.shard_map(
        on_device, mesh=mesh, in_specs=placed, out_specs=P("queue", "space", None), check_vma=False
    )
```

```python
import functools
import math

import jax
import jax.numpy as jnp
from jax import lax
from jax.experimental import pallas as pl
from jax.experimental.pallas import tpu as pltpu
from jax.sharding import PartitionSpec as P

HEAD_DIM = 128
SCALE = 1.0 / math.sqrt(HEAD_DIM)
LOG2E = 1.4426950408889634
MASKED = -1e30
MIB = 1024 * 1024
STEP_HEADS = 4
TAIL = 8
TEMPORAL_FLOPS = 5 * 10**9
QUERY_BLOCK = 720
KEY_BLOCK = 720


def columns(head):
    return slice(head * HEAD_DIM, (head + 1) * HEAD_DIM)


def pack_kernel(q_ref, k_ref, v_ref, out_ref, own_ref, *, main):
    for part, ref in enumerate((k_ref, v_ref)):
        own_ref[part, main:, :] = jnp.zeros_like(own_ref[part, main:, :])
        own_ref[part, : main + 1, :] = ref[0]
    row = lax.broadcasted_iota(jnp.int32, (TAIL, HEAD_DIM), 0)
    for head in range(STEP_HEADS):
        tail = jnp.zeros((TAIL, HEAD_DIM), jnp.float32)
        for part, ref in enumerate((q_ref, k_ref, v_ref)):
            out_ref[head, part * main : (part + 1) * main, :] = ref[0, :main, columns(head)]
            last = ref[0, main : main + 1, columns(head)].astype(jnp.float32)
            tail = jnp.where(row == part, last, tail)
        out_ref[head, 3 * main :, :] = tail.astype(jnp.bfloat16)


def pack(queries, keys, values):
    _, rows, channels = queries.shape
    heads = channels // HEAD_DIM
    main = rows - 1
    total = 3 * main + TAIL
    spec = pl.BlockSpec((1, rows, STEP_HEADS * HEAD_DIM), lambda h: (0, 0, h))
    return pl.pallas_call(
        functools.partial(pack_kernel, main=main),
        grid=(heads // STEP_HEADS,),
        in_specs=[spec] * 3,
        out_specs=[
            pl.BlockSpec((STEP_HEADS, total, HEAD_DIM), lambda h: (h, 0, 0)),
            pl.BlockSpec((2, main + 8, STEP_HEADS * HEAD_DIM), lambda h: (0, 0, h)),
        ],
        out_shape=[
            jax.ShapeDtypeStruct((heads, total, HEAD_DIM), jnp.bfloat16),
            jax.ShapeDtypeStruct((2, main + 8, channels), jnp.bfloat16),
        ],
        cost_estimate=pl.CostEstimate(flops=0, bytes_accessed=8 * queries.size * 2, transcendentals=0),
        name="pack",
    )(queries, keys, values)


def attend_kernel(got_ref, out_ref, q_all, k_all, v_all, o_all, *, sources, main):
    row = lax.broadcasted_iota(jnp.int32, (16, HEAD_DIM), 0)
    tails = [jnp.zeros((16, HEAD_DIM), jnp.float32) for _ in range(3)]
    for s in range(sources):
        at = slice(s * main, (s + 1) * main)
        q_all[at, :] = got_ref[s, :main, :]
        k_all[at, :] = got_ref[s, main : 2 * main, :]
        v_all[at, :HEAD_DIM] = got_ref[s, 2 * main : 3 * main, :]
        tail = got_ref[s, 3 * main :, :].astype(jnp.float32)
        for part in range(3):
            tails[part] = jnp.where(row == s, tail[part : part + 1, :], tails[part])
    end = sources * main
    q_all[end:, :] = tails[0].astype(jnp.bfloat16)
    k_all[end:, :] = tails[1].astype(jnp.bfloat16)
    v_all[end:, :HEAD_DIM] = tails[2].astype(jnp.bfloat16)
    v_all[:, HEAD_DIM:] = jnp.ones((end + 16, HEAD_DIM), jnp.bfloat16)

    def one_block(i, carry):
        rows = pl.ds(pl.multiple_of(i * QUERY_BLOCK, 16), QUERY_BLOCK)
        queries = q_all[rows, :]
        top = summed = None
        for start in range(0, end + 16, KEY_BLOCK):
            keys = slice(start, start + KEY_BLOCK)
            scores = lax.dot_general(
                queries, k_all[keys, :], (((1,), (1,)), ((), ())), preferred_element_type=jnp.float32
            )
            here = jnp.max(scores, axis=1, keepdims=True)
            new_top = here if top is None else jnp.maximum(top, here)
            weights = jnp.exp2((scores - new_top) * (SCALE * LOG2E)).astype(jnp.bfloat16)
            part = jnp.dot(weights, v_all[keys, :], preferred_element_type=jnp.float32)
            summed = part if top is None else summed * jnp.exp2((top - new_top) * (SCALE * LOG2E)) + part
            top = new_top
        o_all[rows, :] = (summed[:, :HEAD_DIM] / summed[:, HEAD_DIM:]).astype(jnp.bfloat16)
        return carry

    lax.fori_loop(0, (end + 16) // QUERY_BLOCK, one_block, 0, unroll=True)
    last = o_all[end:, :].astype(jnp.float32)
    for s in range(sources):
        out_ref[s, :main, :] = o_all[s * main : (s + 1) * main, :]
        out_ref[s, main : main + 1, :] = last[s : s + 1, :].astype(jnp.bfloat16)


def attend(got, rows):
    sources, total, _ = got.shape
    main = rows - 1
    tokens = sources * rows
    return pl.pallas_call(
        functools.partial(attend_kernel, sources=sources, main=main),
        in_specs=[pl.BlockSpec(memory_space=pltpu.VMEM)],
        out_specs=pl.BlockSpec(memory_space=pltpu.VMEM),
        out_shape=jax.ShapeDtypeStruct((sources, rows, HEAD_DIM), jnp.bfloat16),
        scratch_shapes=[
            pltpu.VMEM((tokens, HEAD_DIM), jnp.bfloat16),
            pltpu.VMEM((tokens, HEAD_DIM), jnp.bfloat16),
            pltpu.VMEM((tokens, 2 * HEAD_DIM), jnp.bfloat16),
            pltpu.VMEM((tokens, HEAD_DIM), jnp.bfloat16),
        ],
        compiler_params=pltpu.CompilerParams(vmem_limit_bytes=48 * MIB),
        cost_estimate=pl.CostEstimate(
            flops=4 * tokens * tokens * HEAD_DIM, bytes_accessed=8 * tokens * HEAD_DIM, transcendentals=tokens * tokens
        ),
        name="attend",
    )(got)


def temporal_kernel(usable_ref, q_ref, k_ref, v_ref, near_k_ref, near_v_ref, far_ref, out_ref):
    rows = q_ref.shape[1]
    for head in range(STEP_HEADS):
        at = columns(head)
        q = q_ref[0, :, at].astype(jnp.float32)
        keys = (k_ref[0, :, at], near_k_ref[0, :, at], far_ref[0, :rows, at])
        values = (v_ref[0, :, at], near_v_ref[0, :, at], far_ref[1, :rows, at])
        scores = []
        for j in range(3):
            score = jnp.sum(q * keys[j].astype(jnp.float32), axis=1, keepdims=True) * SCALE
            scores.append(jnp.where(usable_ref[j] > 0, score, MASKED))
        top = jnp.maximum(jnp.maximum(scores[0], scores[1]), scores[2])
        terms = [jnp.exp(score - top) for score in scores]
        total = terms[0] + terms[1] + terms[2]
        summed = jnp.zeros_like(q)
        for j in range(3):
            summed += terms[j].astype(jnp.bfloat16).astype(jnp.float32) * values[j].astype(jnp.float32)
        out_ref[0, :, at] = summed / total


def temporal_attend(usable, queries, keys, values, near_keys, near_values, far):
    _, rows, channels = queries.shape
    width = STEP_HEADS * HEAD_DIM
    spec = pl.BlockSpec((1, rows, width), lambda h: (0, 0, h))
    pair = pl.BlockSpec((2, far.shape[1], width), lambda h: (0, 0, h))
    return pl.pallas_call(
        temporal_kernel,
        grid=(channels // width,),
        in_specs=[pl.BlockSpec(memory_space=pltpu.SMEM)] + [spec] * 5 + [pair],
        out_specs=spec,
        out_shape=jax.ShapeDtypeStruct(queries.shape, jnp.float32),
        cost_estimate=pl.CostEstimate(flops=TEMPORAL_FLOPS, bytes_accessed=18 * queries.size, transcendentals=0),
        name="temporal",
    )(usable, queries, keys, values, near_keys, near_values, far)


def finish_kernel(first_ref, spatial_ref, temporal_ref, residual_ref, gate_ref, fresh_ref, out_ref):
    is_first = first_ref[0] > 0
    for head in range(spatial_ref.shape[0]):
        at = columns(head)
        mixed = (spatial_ref[head].astype(jnp.float32) + temporal_ref[0, :, at]).astype(jnp.bfloat16)
        updated = residual_ref[0, :, at].astype(jnp.float32) + gate_ref[:, at] * mixed.astype(jnp.float32)
        out_ref[0, :, at] = jnp.where(is_first, fresh_ref[:, at].astype(jnp.float32), updated).astype(jnp.bfloat16)


def finish(is_first, spatial, temporal, residual, gate_row, fresh):
    return pl.pallas_call(
        finish_kernel,
        in_specs=[pl.BlockSpec(memory_space=pltpu.SMEM)] + [pl.BlockSpec(memory_space=pltpu.VMEM)] * 5,
        out_specs=pl.BlockSpec(memory_space=pltpu.VMEM),
        out_shape=jax.ShapeDtypeStruct(residual.shape, jnp.bfloat16),
        compiler_params=pltpu.CompilerParams(vmem_limit_bytes=16 * MIB),
        cost_estimate=pl.CostEstimate(flops=4 * residual.size, bytes_accessed=12 * residual.size, transcendentals=0),
        name="finish",
    )(is_first, spatial, temporal, residual, gate_row, fresh)


def on_device(residual, head_queries, head_keys, head_values, levels, window, level_gate, fresh_frame):
    rows = head_queries.shape[1]
    frame = lax.axis_index("queue")
    frames = lax.axis_size("queue")
    near_pairs = [(i, i ^ 1) for i in range(frames)]
    far_pairs = [(i, j) for i, j in ((i, ((i + 1) ^ 1) - 1) for i in range(frames)) if 0 <= j < frames]

    sent, own = pack(head_queries, head_keys, head_values)
    got = lax.all_to_all(sent, "space", split_axis=0, concat_axis=0, tiled=True)
    got, own, window, levels = lax.optimization_barrier((got, own, window, levels))

    far = lax.ppermute(own, "queue", far_pairs)
    before = (window[0, 0] >= 1) & (frame >= 1)
    after = (window[0, 1] >= 1) & (frame <= frames - 2)
    odd = frame % 2 == 1
    near_usable, far_usable = jnp.where(odd, before, after), jnp.where(odd, after, before)
    usable = jnp.stack([jnp.bool_(True), near_usable, far_usable]).astype(jnp.int32)
    is_first = (frame == 0).astype(jnp.int32)[None]
    gate_row = lax.dynamic_slice_in_dim(level_gate, levels[0], 1, axis=0)
    back = attend(got, rows)
    far, head_keys, head_values, _ = lax.optimization_barrier((far, head_keys, head_values, back))

    near_keys = lax.ppermute(head_keys, "queue", near_pairs)
    near_values = lax.ppermute(head_values, "queue", near_pairs)
    temporal = temporal_attend(usable, head_queries, head_keys, head_values, near_keys, near_values, far)
    spatial = lax.all_to_all(back, "space", split_axis=0, concat_axis=0, tiled=True)
    updated = finish(is_first, spatial, temporal, residual, gate_row, fresh_frame)
    return lax.ppermute(updated, "queue", [(i, (i - 1) % frames) for i in range(frames)])


def solution(mesh):
    placed = (
        P("queue", "space", None),
        P("queue", "space", None),
        P("queue", "space", None),
        P("queue", "space", None),
        P("queue"),
        P("queue", None),
        P(),
        P("space", None),
    )
    return jax.shard_map(
        on_device, mesh=mesh, in_specs=placed, out_specs=P("queue", "space", None), check_vma=False
    )
```

```python
import functools
import math

import jax
import jax.numpy as jnp
from jax import lax
from jax.experimental import pallas as pl
from jax.experimental.pallas import tpu as pltpu
from jax.sharding import PartitionSpec as P

HEAD_DIM = 128
SCALE = 1.0 / math.sqrt(HEAD_DIM)
LOG2E = 1.4426950408889634
MASKED = -1e30
MIB = 1024 * 1024
STEP_HEADS = 4
TAIL = 8
TEMPORAL_FLOPS = 5 * 10**9
QUERY_BLOCK = 720
KEY_BLOCK = 720


def columns(head):
    return slice(head * HEAD_DIM, (head + 1) * HEAD_DIM)


def pack_kernel(q_ref, k_ref, v_ref, out_ref, own_ref, *, main):
    for part, ref in enumerate((k_ref, v_ref)):
        own_ref[part, main:, :] = jnp.zeros_like(own_ref[part, main:, :])
        own_ref[part, : main + 1, :] = ref[0]
    row = lax.broadcasted_iota(jnp.int32, (TAIL, HEAD_DIM), 0)
    for head in range(STEP_HEADS):
        tail = jnp.zeros((TAIL, HEAD_DIM), jnp.float32)
        for part, ref in enumerate((q_ref, k_ref, v_ref)):
            out_ref[head, part * main : (part + 1) * main, :] = ref[0, :main, columns(head)]
            last = ref[0, main : main + 1, columns(head)].astype(jnp.float32)
            tail = jnp.where(row == part, last, tail)
        out_ref[head, 3 * main :, :] = tail.astype(jnp.bfloat16)


def pack(queries, keys, values):
    _, rows, channels = queries.shape
    heads = channels // HEAD_DIM
    main = rows - 1
    total = 3 * main + TAIL
    spec = pl.BlockSpec((1, rows, STEP_HEADS * HEAD_DIM), lambda h: (0, 0, h))
    return pl.pallas_call(
        functools.partial(pack_kernel, main=main),
        grid=(heads // STEP_HEADS,),
        in_specs=[spec] * 3,
        out_specs=[
            pl.BlockSpec((STEP_HEADS, total, HEAD_DIM), lambda h: (h, 0, 0)),
            pl.BlockSpec((2, main + 8, STEP_HEADS * HEAD_DIM), lambda h: (0, 0, h)),
        ],
        out_shape=[
            jax.ShapeDtypeStruct((heads, total, HEAD_DIM), jnp.bfloat16),
            jax.ShapeDtypeStruct((2, main + 8, channels), jnp.bfloat16),
        ],
        cost_estimate=pl.CostEstimate(flops=0, bytes_accessed=8 * queries.size * 2, transcendentals=0),
        name="pack",
    )(queries, keys, values)


def attend_kernel(got_ref, out_ref, q_all, k_all, v_all, o_all, *, sources, main):
    row = lax.broadcasted_iota(jnp.int32, (16, HEAD_DIM), 0)
    tails = [jnp.zeros((16, HEAD_DIM), jnp.float32) for _ in range(3)]
    for s in range(sources):
        at = slice(s * main, (s + 1) * main)
        q_all[at, :] = got_ref[s, :main, :]
        k_all[at, :] = got_ref[s, main : 2 * main, :]
        v_all[at, :HEAD_DIM] = got_ref[s, 2 * main : 3 * main, :]
        tail = got_ref[s, 3 * main :, :].astype(jnp.float32)
        for part in range(3):
            tails[part] = jnp.where(row == s, tail[part : part + 1, :], tails[part])
    end = sources * main
    q_all[end:, :] = tails[0].astype(jnp.bfloat16)
    k_all[end:, :] = tails[1].astype(jnp.bfloat16)
    v_all[end:, :HEAD_DIM] = tails[2].astype(jnp.bfloat16)
    v_all[:, HEAD_DIM:] = jnp.ones((end + 16, HEAD_DIM), jnp.bfloat16)

    def one_block(i, carry):
        rows = pl.ds(pl.multiple_of(i * QUERY_BLOCK, 16), QUERY_BLOCK)
        queries = q_all[rows, :]
        top = summed = None
        for start in range(0, end + 16, KEY_BLOCK):
            keys = slice(start, start + KEY_BLOCK)
            scores = lax.dot_general(
                queries, k_all[keys, :], (((1,), (1,)), ((), ())), preferred_element_type=jnp.float32
            )
            here = jnp.max(scores, axis=1, keepdims=True)
            new_top = here if top is None else jnp.maximum(top, here)
            weights = jnp.exp2((scores - new_top) * (SCALE * LOG2E)).astype(jnp.bfloat16)
            part = jnp.dot(weights, v_all[keys, :], preferred_element_type=jnp.float32)
            summed = part if top is None else summed * jnp.exp2((top - new_top) * (SCALE * LOG2E)) + part
            top = new_top
        o_all[rows, :] = (summed[:, :HEAD_DIM] / summed[:, HEAD_DIM:]).astype(jnp.bfloat16)
        return carry

    lax.fori_loop(0, (end + 16) // QUERY_BLOCK, one_block, 0, unroll=True)
    last = o_all[end:, :].astype(jnp.float32)
    for s in range(sources):
        out_ref[s, :main, :] = o_all[s * main : (s + 1) * main, :]
        out_ref[s, main : main + 1, :] = last[s : s + 1, :].astype(jnp.bfloat16)


def attend(got, rows):
    sources, total, _ = got.shape
    main = rows - 1
    tokens = sources * rows
    return pl.pallas_call(
        functools.partial(attend_kernel, sources=sources, main=main),
        in_specs=[pl.BlockSpec(memory_space=pltpu.VMEM)],
        out_specs=pl.BlockSpec(memory_space=pltpu.VMEM),
        out_shape=jax.ShapeDtypeStruct((sources, rows, HEAD_DIM), jnp.bfloat16),
        scratch_shapes=[
            pltpu.VMEM((tokens, HEAD_DIM), jnp.bfloat16),
            pltpu.VMEM((tokens, HEAD_DIM), jnp.bfloat16),
            pltpu.VMEM((tokens, 2 * HEAD_DIM), jnp.bfloat16),
            pltpu.VMEM((tokens, HEAD_DIM), jnp.bfloat16),
        ],
        compiler_params=pltpu.CompilerParams(vmem_limit_bytes=48 * MIB),
        cost_estimate=pl.CostEstimate(
            flops=4 * tokens * tokens * HEAD_DIM, bytes_accessed=8 * tokens * HEAD_DIM, transcendentals=tokens * tokens
        ),
        name="attend",
    )(got)


def temporal_kernel(usable_ref, q_ref, k_ref, v_ref, near_k_ref, near_v_ref, far_ref, residual_ref, fresh_ref, gate_ref, out_ref):
    rows = q_ref.shape[1]
    for head in range(STEP_HEADS):
        at = columns(head)
        q = q_ref[0, :, at].astype(jnp.float32)
        keys = (k_ref[0, :, at], near_k_ref[0, :, at], far_ref[0, :rows, at])
        values = (v_ref[0, :, at], near_v_ref[0, :, at], far_ref[1, :rows, at])
        scores = []
        for j in range(3):
            score = jnp.sum(q * keys[j].astype(jnp.float32), axis=1, keepdims=True) * SCALE
            scores.append(jnp.where(usable_ref[j] > 0, score, MASKED))
        top = jnp.maximum(jnp.maximum(scores[0], scores[1]), scores[2])
        terms = [jnp.exp(score - top) for score in scores]
        total = terms[0] + terms[1] + terms[2]
        summed = jnp.zeros_like(q)
        for j in range(3):
            summed += terms[j].astype(jnp.bfloat16).astype(jnp.float32) * values[j].astype(jnp.float32)
        base = jnp.where(usable_ref[3] > 0, fresh_ref[:, at].astype(jnp.float32), residual_ref[0, :, at].astype(jnp.float32))
        out_ref[0, :, at] = base + gate_ref[:, at] * (summed / total)


def temporal_attend(usable, queries, keys, values, near_keys, near_values, far, residual, fresh, gate_row):
    _, rows, channels = queries.shape
    width = STEP_HEADS * HEAD_DIM
    spec = pl.BlockSpec((1, rows, width), lambda h: (0, 0, h))
    pair = pl.BlockSpec((2, far.shape[1], width), lambda h: (0, 0, h))
    return pl.pallas_call(
        temporal_kernel,
        grid=(channels // width,),
        in_specs=[pl.BlockSpec(memory_space=pltpu.SMEM)] + [spec] * 5
        + [pair, spec, pl.BlockSpec((rows, width), lambda h: (0, h)), pl.BlockSpec((1, width), lambda h: (0, h))],
        out_specs=spec,
        out_shape=jax.ShapeDtypeStruct(queries.shape, jnp.float32),
        cost_estimate=pl.CostEstimate(flops=TEMPORAL_FLOPS, bytes_accessed=18 * queries.size, transcendentals=0),
        name="temporal",
    )(usable, queries, keys, values, near_keys, near_values, far, residual, fresh, gate_row)


def finish_kernel(spatial_ref, base_ref, gate_ref, out_ref):
    for head in range(spatial_ref.shape[0]):
        at = columns(head)
        updated = base_ref[0, :, at] + gate_ref[:, at] * spatial_ref[head].astype(jnp.float32)
        out_ref[0, :, at] = updated.astype(jnp.bfloat16)


def finish(spatial, base, gate_row):
    return pl.pallas_call(
        finish_kernel,
        in_specs=[pl.BlockSpec(memory_space=pltpu.VMEM)] * 3,
        out_specs=pl.BlockSpec(memory_space=pltpu.VMEM),
        out_shape=jax.ShapeDtypeStruct(base.shape, jnp.bfloat16),
        compiler_params=pltpu.CompilerParams(vmem_limit_bytes=16 * MIB),
        cost_estimate=pl.CostEstimate(flops=4 * base.size, bytes_accessed=8 * base.size, transcendentals=0),
        name="finish",
    )(spatial, base, gate_row)


def on_device(residual, head_queries, head_keys, head_values, levels, window, level_gate, fresh_frame):
    rows = head_queries.shape[1]
    frame = lax.axis_index("queue")
    frames = lax.axis_size("queue")
    near_pairs = [(i, i ^ 1) for i in range(frames)]
    far_pairs = [(i, j) for i, j in ((i, ((i + 1) ^ 1) - 1) for i in range(frames)) if 0 <= j < frames]

    sent, own = pack(head_queries, head_keys, head_values)
    got = lax.all_to_all(sent, "space", split_axis=0, concat_axis=0, tiled=True)
    got, own, window, levels = lax.optimization_barrier((got, own, window, levels))

    far = lax.ppermute(own, "queue", far_pairs)
    before = (window[0, 0] >= 1) & (frame >= 1)
    after = (window[0, 1] >= 1) & (frame <= frames - 2)
    odd = frame % 2 == 1
    near_usable, far_usable = jnp.where(odd, before, after), jnp.where(odd, after, before)
    is_first = frame == 0
    usable = jnp.stack([jnp.bool_(True), near_usable, far_usable, is_first]).astype(jnp.int32)
    gate_row = jnp.where(is_first, 0.0, lax.dynamic_slice_in_dim(level_gate, levels[0], 1, axis=0))
    back = attend(got, rows)
    far, head_keys, head_values, _ = lax.optimization_barrier((far, head_keys, head_values, back))

    near_keys = lax.ppermute(head_keys, "queue", near_pairs)
    near_values = lax.ppermute(head_values, "queue", near_pairs)
    base = temporal_attend(
        usable, head_queries, head_keys, head_values, near_keys, near_values, far, residual, fresh_frame, gate_row
    )
    spatial = lax.all_to_all(back, "space", split_axis=0, concat_axis=0, tiled=True)
    updated = finish(spatial, base, gate_row)
    return lax.ppermute(updated, "queue", [(i, (i - 1) % frames) for i in range(frames)])


def solution(mesh):
    placed = (
        P("queue", "space", None),
        P("queue", "space", None),
        P("queue", "space", None),
        P("queue", "space", None),
        P("queue"),
        P("queue", None),
        P(),
        P("space", None),
    )
    return jax.shard_map(
        on_device, mesh=mesh, in_specs=placed, out_specs=P("queue", "space", None), check_vma=False
    )
```
